512 devices in a mesh: prow: 32 (over y, x), pcol: 16 (over z, core).
Axes of the slice: x: 4, y: 8, z: 8, core: 2. Of those that a mesh axis runs over, the one named last changes fastest.
Arguments:
- panel_transposed: float32 [2, 512, 12288], P(None, 'pcol', 'prow'), may hold values from -0.75 to 0.75
- inverse_transposed: float32 [2, 512, 512], P(None, 'pcol'), as said below
- targets: int32 [2, 96], replicated, may hold values from 0 to 127, as said below
Outputs:
- updates: float32 [16384, 16384], P('prow', 'pcol')
The draws below stay inside these ranges and needn't reach their ends.
Inputs may be any that keep to these rules, and one draw needn't show every extreme that they name: Along each panel the targets rise strictly. Row block i lies on prow index i // 3; its target's owner, targets // 4, is that index or the one before it. The first row block targets 0 and the last targets 128 - 1. `inverse_transposed`: upper triangular with a positive diagonal.
All inputs are finite; a program needn't handle non-finite values.
Results may differ from the reference program's by a relative error of at most 0.000086.
Values sent between devices are 32-bit elements; how exact they have to be, the bound alone decides.
No kernel may reach another device: no remote copies, remote signals or barrier semaphores. Data moves between devices by JAX's collectives and lax.ppermute only.
A program may use at most 64 MiB of HBM per device.

```python
import math
import jax
import jax.numpy as jnp
from jax import lax

PANEL_WIDTH = 512
BLOCK = 128
ROW_BLOCKS = 3
PANEL_BLOCKS = 96
ANC_BLOCKS = 128


def draw_targets(key, part):
    key = jax.random.fold_in(key, 7)
    key_skip, key_last = jax.random.split(key)
    owners = PANEL_BLOCKS // ROW_BLOCKS
    owner_ids = jnp.arange(owners, dtype=jnp.int32)
    base = 4 * owner_ids
    skipped = jax.random.randint(key_skip, (2, owners), 0, 3, dtype=jnp.int32)
    first = jnp.where(owner_ids == 0, 0, base - 1)
    middle = base + jnp.where(skipped > 0, 0, 1)
    final = base + jnp.where(skipped < 2, 2, 1)
    middle = jnp.where(owner_ids[None, :] == 0, 1, middle)
    final = jnp.where(owner_ids[None, :] == 0, 2, final)
    last_mid = base[owners - 1] + jax.random.randint(key_last, (2,), 0, 3, dtype=jnp.int32)
    middle = middle.at[:, owners - 1].set(last_mid)
    final = final.at[:, owners - 1].set(ANC_BLOCKS - 1)
    first = jnp.broadcast_to(first[None, :], (2, owners))
    stacked = jnp.stack([first, middle, final], axis=2)
    return stacked.reshape(2, PANEL_BLOCKS).astype(jnp.int32)


def draw_inverse_transposed(key, part):
    key = jax.random.fold_in(key, 11)
    key_diag, key_beyond = jax.random.split(key)
    row_ids = jnp.arange(PANEL_WIDTH)[:, None]
    col_ids = jnp.arange(PANEL_WIDTH)[None, :]
    diagonal = jnp.exp(jax.random.uniform(key_diag, (2, PANEL_WIDTH), jnp.float32, math.log(0.5), math.log(2.0)))
    beyond = jax.random.normal(key_beyond, (2, PANEL_WIDTH, PANEL_WIDTH), jnp.float32)
    beyond = beyond * (0.5 / jnp.sqrt(col_ids.astype(jnp.float32) + 1.0))
    strict = jnp.where(row_ids < col_ids, beyond, 0.0)
    onto = jnp.where(row_ids == col_ids, 1.0, 0.0)[None, :, :] * diagonal[:, None, :]
    return (strict + onto).astype(jnp.float32)


def level_of(rng, extent, pieces, low, top_value):
    def one(axis_at, shards_of):
        heights = jax.random.uniform(jax.random.fold_in(jax.random.fold_in(rng, 6), axis_at), (shards_of,), jnp.float32, low / len(pieces), top_value / len(pieces))
        return jnp.repeat(jnp.exp(heights), extent[axis_at] // shards_of).reshape((-1,) + (1,) * (len(extent) - axis_at - 1))

    loudness = one(*pieces[0])
    for cut in pieces[1:]:
        loudness = loudness * one(*cut)
    return loudness


def noise(stream_key, extent, deviation, reach, shards=(), kind=jnp.bfloat16):
    array = jax.random.normal(stream_key, extent, jnp.float32) * deviation
    if len(shards) > 0:
        array = level_of(stream_key, extent, shards, -0.22, 0.18) * array
    return jnp.clip(array, min=-reach, max=reach).astype(kind)


def setup_inputs(seed: int = 0) -> dict:
    key_of = jax.random.split(jax.random.key(seed), 4)
    return {
        "panel_transposed": noise(key_of[0], (2, PANEL_WIDTH, PANEL_BLOCKS * BLOCK), 0.125, 0.75, ((1, 16), (2, 32)), jnp.float32),
        "inverse_transposed": draw_inverse_transposed(jax.random.fold_in(key_of[3], 71), 0),
        "targets": draw_targets(jax.random.fold_in(key_of[3], 71), 0),
    }


def reference(panel_transposed, inverse_transposed, targets):
    cholesky_factor = jnp.einsum('yqg,yqz->ygz', inverse_transposed, panel_transposed, precision=lax.Precision.HIGHEST)
    block_list = cholesky_factor.reshape(2, PANEL_WIDTH, PANEL_BLOCKS, BLOCK)
    placed = []
    for which_panel in range(2):
        spread = jnp.zeros((PANEL_WIDTH, ANC_BLOCKS, BLOCK), cholesky_factor.dtype)
        spread = spread.at[:, targets[which_panel], :].set(block_list[which_panel])
        placed.append(spread.reshape(PANEL_WIDTH, ANC_BLOCKS * BLOCK))
    stacked = jnp.stack(placed).reshape(2 * PANEL_WIDTH, ANC_BLOCKS * BLOCK)
    return jnp.dot(stacked.T, stacked, precision=lax.Precision.HIGHEST, preferred_element_type=jnp.float32)
```

```python
import functools
import jax
import jax.numpy as jnp
from jax import lax
from jax.experimental import pallas as pl
from jax.experimental.pallas import tpu as pltpu
from jax.sharding import PartitionSpec as P

BLOCK = 128
NX, NZ, NC = 4, 8, 2
AXES = ("prow", "pcol")
F32, BF16 = jnp.float32, jnp.bfloat16
MIB = 1 << 20
PIECE_OFFSETS = (0, 4, -1, 3, 1, -3, -2, 2)


def device(y, x, z, core):
    return ((y % 8) * NX + x) * NZ * NC + z * NC + core


def every():
    for y in range(8):
        for x in range(NX):
            for z in range(NZ):
                for core in range(NC):
                    yield y, x, z, core


def transposing(lift):
    return [(device(y, x, z, k), device(2 * y - z + lift, x, y, k)) for y, x, z, k in every()]


def along_y(distance):
    return [(device(y + distance, x, z, k), device(y, x, z, k)) for y, x, z, k in every()]


def to_columns():
    first, second, sibling, relay_home, relay_other = [], [], [], [], []
    for y, x, z, k in every():
        here = device(y, x, z, k)
        wanted_by = x // 2
        near, across = device(y, x ^ 1, z, wanted_by), device(y, 3 - x, z, wanted_by)
        first.append((here, near if k == 0 else across))
        second.append((here, across if k == 0 else near))
        if wanted_by == k:
            relay_home.append((here, device(y, 3 - x, z, k)))
        else:
            sibling.append((here, device(y, x, z, 1 - k)))
            relay_other.append((here, device(y, x ^ 1, z, k)))
    return first, second, sibling, relay_home, relay_other


def send(value, pairs):
    return lax.ppermute(value, AXES, pairs)


def split(value):
    high = value.astype(BF16)
    return high, (value - high.astype(F32)).astype(BF16)


def dot3(a, b, dims):
    (a_high, a_low), (b_high, b_low) = a, b
    mul = functools.partial(lax.dot_general, dimension_numbers=(dims, ((), ())), preferred_element_type=F32)
    return mul(a_high, b_high) + (mul(a_high, b_low) + mul(a_low, b_high))


def place_kernel(row_ref, targets_ref, own_ref, next_ref, inverse_ref, placed_ref, both_ref):
    row = row_ref[0]
    blocks = 3
    count = targets_ref.shape[1]
    for panel in range(2):
        for slot in range(4):
            total = jnp.zeros((own_ref.shape[1], BLOCK), F32)
            for source in range(2 * blocks):
                index = row * blocks + source
                target = targets_ref[panel, jnp.minimum(index, count - 1)]
                hit = jnp.logical_and(index < count, target == row * 4 + slot)
                ref = own_ref if source < blocks else next_ref
                at = (source % blocks) * BLOCK
                total = jnp.where(hit, ref[panel, :, at : at + BLOCK], total)
            placed_ref[panel, :, slot * BLOCK : (slot + 1) * BLOCK] = total
            both_ref[panel, :, slot * BLOCK : (slot + 1) * BLOCK] = total
        both_ref[2 + panel] = inverse_ref[panel]


def rows_kernel(gathered_ref, inv_high, inv_low, row_high, row_low):
    for panel in range(2):
        inverse = gathered_ref[:, 2 + panel].reshape(512, 512)
        rows = gathered_ref[:, panel].reshape(512, 512)
        factor = dot3(split(inverse), split(rows), ((0,), (0,)))
        row_high[panel], row_low[panel] = split(factor.T)
        inv_high[panel], inv_low[panel] = split(inverse.T)


def columns_kernel(
    info, inv_high, inv_low, row_high, row_low, own, first, second, sibling, relay_a, relay_b, out, high, low
):
    home = info[0] == 1
    at_a = pl.multiple_of(info[1] * 512, 512)
    at_b = pl.multiple_of(512 - info[1] * 512, 512)

    def unpack(piece, _):
        z = info[8 + piece]
        for half, refs, at in ((2, (first,), at_a), (3, (second,), at_a), (4, (own, relay_a), at_b), (5, (sibling, relay_b), at_b)):
            start = pl.multiple_of(z * 64 + info[half] * 32, 32)
            for panel in range(2):
                value = refs[0][piece, panel]
                if len(refs) == 2:
                    value = jnp.where(home, value, refs[1][piece, panel])
                value_high, value_low = split(value)
                high[panel, pl.ds(start, 32), pl.ds(at, 512)] = value_high
                low[panel, pl.ds(start, 32), pl.ds(at, 512)] = value_low
        return 0

    lax.fori_loop(0, 8, unpack, 0)

    def tile(step, _):
        at = pl.multiple_of(step * 256, 256)
        total = None
        for panel in range(2):
            cols = (high[panel, :, pl.ds(at, 256)], low[panel, :, pl.ds(at, 256)])
            factor = dot3((inv_high[panel], inv_low[panel]), cols, ((1,), (0,)))
            part = dot3((row_high[panel], row_low[panel]), split(factor), ((1,), (0,)))
            total = part if total is None else total + part
        out[:, pl.ds(at, 256)] = total
        return 0

    lax.fori_loop(0, 4, tile, 0)


VMEM = pl.BlockSpec(memory_space=pltpu.VMEM)
SMEM = pl.BlockSpec(memory_space=pltpu.SMEM)


def body(panel, inverse, targets):
    row, col = lax.axis_index("prow"), lax.axis_index("pcol")
    y, x, z, core = row // NX, row % NX, col // NC, col % NC

    following = send(panel, [(r * 16 + c, (r - 1) * 16 + c) for r in range(1, 32) for c in range(16)])
    placed, both = pl.pallas_call(
        place_kernel,
        out_shape=(jax.ShapeDtypeStruct((2, 32, 512), F32), jax.ShapeDtypeStruct((4, 32, 512), F32)),
        in_specs=[SMEM, SMEM, VMEM, VMEM, VMEM],
        out_specs=(VMEM, VMEM),
        name="place",
    )(row.reshape(1), targets, panel, following, inverse)

    gathered = lax.all_gather(both, "pcol")

    low_piece, high_piece = send(placed, transposing(0)), send(placed, transposing(4))
    pair = jnp.stack([low_piece, high_piece])
    up, down = send(pair, along_y(1)), send(pair, along_y(-1))
    up2, down2 = send(low_piece, along_y(2)), send(low_piece, along_y(-2))
    own = jnp.concatenate([pair, up, down, up2[None], down2[None]])

    p_first, p_second, p_sibling, p_home, p_other = to_columns()
    first, second, sibling = send(own, p_first), send(own, p_second), send(own, p_sibling)
    relay_a, relay_b = send(first, p_home), send(first, p_other)

    weights = jax.ShapeDtypeStruct((2, 512, 512), BF16)
    inv_high, inv_low, row_high, row_low = pl.pallas_call(
        rows_kernel,
        out_shape=(weights,) * 4,
        in_specs=[VMEM],
        out_specs=(VMEM,) * 4,
        compiler_params=pltpu.CompilerParams(vmem_limit_bytes=40 * MIB),
        cost_estimate=pl.CostEstimate(flops=2 * 3 * 2 * 512**3, bytes_accessed=8 * MIB, transcendentals=0),
        name="rows",
    )(gathered)

    is_home = (x // 2 == core).astype(jnp.int32)
    near = jnp.where(is_home == 1, x ^ 1, 3 - x)
    info = jnp.stack(
        [
            is_home,
            near - 2 * core,
            1 - is_home,
            is_home,
            jnp.where(is_home == 1, core, 0),
            jnp.where(is_home == 1, 1 - core, 1),
            0 * core,
            0 * core,
        ]
    )
    info = jnp.concatenate([info, (2 * z - y + jnp.array(PIECE_OFFSETS, jnp.int32)) % 8])
    return pl.pallas_call(
        columns_kernel,
        out_shape=jax.ShapeDtypeStruct((512, 1024), F32),
        in_specs=[SMEM] + [VMEM] * 10,
        out_specs=VMEM,
        scratch_shapes=[pltpu.VMEM((2, 512, 1024), BF16), pltpu.VMEM((2, 512, 1024), BF16)],
        compiler_params=pltpu.CompilerParams(vmem_limit_bytes=48 * MIB),
        cost_estimate=pl.CostEstimate(flops=2 * 3 * 4 * 512 * 512 * 1024, bytes_accessed=12 * MIB, transcendentals=0),
        name="columns",
    )(info, inv_high, inv_low, row_high, row_low, own, first, second, sibling, relay_a, relay_b)


def solution(mesh):
    specs = (P(None, "pcol", "prow"), P(None, "pcol", None), P())
    return jax.shard_map(body, mesh=mesh, in_specs=specs, out_specs=P("prow", "pcol"), check_vma=False)
```

```python
import functools
import jax
import jax.numpy as jnp
from jax import lax
from jax.experimental import pallas as pl
from jax.experimental.pallas import tpu as pltpu
from jax.sharding import PartitionSpec as P

BLOCK = 128
NX, NZ, NC = 4, 8, 2
AXES = ("prow", "pcol")
F32, BF16 = jnp.float32, jnp.bfloat16
MIB = 1 << 20
LIFTS = ((0, 4), (2, 6))
OWNER, GROUP = (0, 1, 1, 0), (0, 0, 1, 1)


def device(y, x, z, core):
    return ((y % 8) * NX + x % NX) * NZ * NC + z * NC + core


def every():
    for y in range(8):
        for x in range(NX):
            for z in range(NZ):
                for core in range(NC):
                    yield y, x, z, core


def moved(down_y=0, right_x=0, flip=0):
    return [(device(y, x, z, k), device(y - down_y, x + right_x, z, k ^ flip)) for y, x, z, k in every()]


def to_sibling():
    return moved(flip=1)


def to_previous_row(flip):
    rows, cols = 8 * NX, NZ * NC
    return [(r * cols + c, (r - 1) * cols + (c ^ flip)) for r in range(1, rows) for c in range(cols)]


def transposing(which):
    pairs = []
    for y, x, z, k in every():
        place = [i for i in range(4) if (OWNER[i], GROUP[i]) == (x % 2, k)][0]
        pairs.append((device(y, x, z, k), device(z - y + LIFTS[k][which], place - 2 * (x // 2), y, x // 2)))
    return pairs


def send(value, pairs):
    return lax.ppermute(value, AXES, pairs)


def split(value):
    high = value.astype(BF16)
    return high, (value - high.astype(F32)).astype(BF16)


def dot3(a, b, dims):
    (a_high, a_low), (b_high, b_low) = a, b
    mul = functools.partial(lax.dot_general, dimension_numbers=(dims, ((), ())), preferred_element_type=F32)
    return mul(a_high, b_high) + (mul(a_high, b_low) + mul(a_low, b_high))


def place_kernel(row_ref, targets_ref, own, following, sibling_own, sibling_following, inverse, pieces, both):
    row = row_ref[0]
    blocks = 3
    count = targets_ref.shape[1]
    for panel in range(2):
        for slot in range(4):
            into = slice(slot * BLOCK, (slot + 1) * BLOCK)
            hits = []
            for source in range(2 * blocks):
                index = row * blocks + source
                target = targets_ref[panel, jnp.minimum(index, count - 1)]
                hits.append(jnp.logical_and(index < count, target == row * 4 + slot))
            for core, refs in enumerate(((own, following), (sibling_own, sibling_following))):
                total = jnp.zeros((own.shape[1], BLOCK), F32)
                for source, hit in enumerate(hits):
                    at = (source % blocks) * BLOCK
                    total = jnp.where(hit, refs[source // blocks][panel, :, at : at + BLOCK], total)
                pieces[core, panel, :, into] = total
                if core == 0:
                    both[panel, :, into] = total
        both[2 + panel] = inverse[panel]


def rows_kernel(info, gathered_ref, high, low, scales, weight, scale):
    for panel in range(2):
        inverse = gathered_ref[:, 2 + panel].reshape(512, 512)
        rows = gathered_ref[:, panel].reshape(512, 512)
        factor = dot3(split(inverse), split(rows), ((0,), (0,)))
        largest = jnp.max(jnp.abs(inverse), axis=1, keepdims=True)
        weight[panel] = dot3(split(inverse / largest), split(factor), ((1,), (0,)))
        scale[panel] = jnp.broadcast_to(largest, (512, BLOCK))
    for chunk in range(2):
        for group in range(2):
            pieces = []
            for which in range(2):
                for core in (group, 1 - group):
                    start = pl.multiple_of(info[8 + chunk * 4 + group * 2 + which] * 64 + core * 32, 32)
                    for panel in range(2):
                        into = len(pieces) * 32
                        pieces.append(weight[panel, pl.ds(start, 32), :])
                        scales[chunk, group, into : into + 32, :] = scale[panel, pl.ds(start, 32), :]
            high[chunk, group], low[chunk, group] = split(jnp.concatenate(pieces).T)


def product(value, at, high, low, scale):
    scaled = value.reshape(256, 512) * jnp.concatenate([scale[at]] * 4, axis=1)
    return dot3((high[at], low[at]), split(scaled), ((1,), (0,)))


def part(info, chunk, at, value, weights):
    return product(value[...], (chunk, info[4 + at]), *weights)


def add_to(out, info, at, value):
    where = pl.multiple_of(info[at] * 512, 512)
    out[:, pl.ds(where, 512)] += value


def first_kernel(info, high, low, scale, mine, left, right, across, out):
    out[...] = jnp.zeros(out.shape, F32)
    for at, value in enumerate((mine, left, right, across)):
        add_to(out, info, at, part(info, 0, at, value, (high, low, scale)))


def near_kernel(info, high, low, scale, mine, left, right, begun, out):
    out[...] = begun[...]
    for at, value in enumerate((mine, left, right)):
        add_to(out, info, at, part(info, 1, at, value, (high, low, scale)))


def last_kernel(info, high, low, scale, across, near, out):
    out[...] = near[...]
    add_to(out, info, 3, part(info, 1, 3, across, (high, low, scale)))


def after_kernel(*refs):
    pass


def after(value, *others):
    anywhere = pl.BlockSpec(memory_space=pl.ANY)
    return pl.pallas_call(
        after_kernel,
        out_shape=jax.ShapeDtypeStruct(value.shape, value.dtype),
        in_specs=[anywhere] * (1 + len(others)),
        out_specs=anywhere,
        input_output_aliases={0: 0},
        name="after",
    )(value, *others)


VMEM = pl.BlockSpec(memory_space=pltpu.VMEM)
SMEM = pl.BlockSpec(memory_space=pltpu.SMEM)


def body(panel, inverse, targets):
    row, col = lax.axis_index("prow"), lax.axis_index("pcol")
    y, x, z, core = row // NX, row % NX, col // NC, col % NC

    pieces, both = pl.pallas_call(
        place_kernel,
        out_shape=(jax.ShapeDtypeStruct((2, 2, 32, 512), F32), jax.ShapeDtypeStruct((4, 32, 512), F32)),
        in_specs=[SMEM] * 2 + [VMEM] * 5,
        out_specs=(VMEM, VMEM),
        name="place",
    )(
        row.reshape(1),
        targets,
        panel,
        send(panel, to_previous_row(0)),
        send(panel, to_sibling()),
        send(panel, to_previous_row(1)),
        inverse,
    )

    gathered = lax.all_gather(both, "pcol")

    to_right, to_left = moved(right_x=1), moved(right_x=-1)
    mine = jnp.stack([send(pieces, transposing(0)), send(pieces, transposing(1))])
    late = send(mine, moved(down_y=1))
    left, right = send(mine, to_right), send(mine, to_left)
    across = send(left, to_right)
    late_left, late_right = send(late, to_right), send(late, to_left)
    late_across = send(late_right, to_left)

    holders = (x + 2 * core + jnp.array([0, -1, 1, 2], jnp.int32)) % 4
    sources = jnp.array([chunk - lift for chunk in range(2) for lift in LIFTS[0] + LIFTS[1]], jnp.int32)
    info = jnp.concatenate([(holders + 1) // 2 % 2, holders // 2, (y + z + sources) % 8])

    def kernel(run, out_shape, operands, gflop, name, scratch=()):
        return pl.pallas_call(
            run,
            out_shape=out_shape,
            in_specs=[SMEM] + [VMEM] * len(operands),
            out_specs=(VMEM,) * len(out_shape) if isinstance(out_shape, tuple) else VMEM,
            scratch_shapes=scratch,
            compiler_params=pltpu.CompilerParams(vmem_limit_bytes=28 * MIB),
            cost_estimate=pl.CostEstimate(flops=int(gflop * 1e9), bytes_accessed=4 * MIB, transcendentals=0),
            name=name,
        )(info, *operands)

    halves = jax.ShapeDtypeStruct((2, 2, 512, 256), BF16)
    scratch = [pltpu.VMEM((2, 512, 512), F32), pltpu.VMEM((2, 512, BLOCK), F32)]
    made = (halves, halves, jax.ShapeDtypeStruct((2, 2, 256, BLOCK), F32))
    weights = kernel(rows_kernel, made, (gathered,), 3.2, "rows", scratch)

    result = jax.ShapeDtypeStruct((512, 1024), F32)
    total = kernel(first_kernel, result, weights + (mine, left, right, across), 1.6, "first")
    total = kernel(near_kernel, result, weights + (late, late_left, late_right, total), 1.2, "near")
    return kernel(last_kernel, result, weights + (late_across, total), 0.4, "last")


def solution(mesh):
    specs = (P(None, "pcol", "prow"), P(None, "pcol", None), P())
    return jax.shard_map(body, mesh=mesh, in_specs=specs, out_specs=P("prow", "pcol"), check_vma=False)
```

```python
import functools
import jax
import jax.numpy as jnp
from jax import lax
from jax.experimental import pallas as pl
from jax.experimental.pallas import tpu as pltpu
from jax.sharding import PartitionSpec as P

BLOCK = 128
NX, NZ, NC = 4, 8, 2
AXES = ("prow", "pcol")
F32, BF16 = jnp.float32, jnp.bfloat16
MIB = 1 << 20
LIFTS = ((0, 4), (2, 6))
OWNER, GROUP = (0, 1, 1, 0), (0, 0, 1, 1)


def device(y, x, z, core):
    return ((y % 8) * NX + x % NX) * NZ * NC + z * NC + core


def every():
    for y in range(8):
        for x in range(NX):
            for z in range(NZ):
                for core in range(NC):
                    yield y, x, z, core


def swapped(x_of):
    return [(device(y, x, z, k), device(y, x_of(x), z, k)) for y, x, z, k in every()]


def from_y(distance):
    return [(device(y + distance, x, z, k), device(y, x, z, k)) for y, x, z, k in every()]


def to_sibling():
    return [(device(y, x, z, k), device(y, x, z, 1 - k)) for y, x, z, k in every()]


def to_previous_row(flip):
    rows, cols = 8 * NX, NZ * NC
    return [(r * cols + c, (r - 1) * cols + (c ^ flip)) for r in range(1, rows) for c in range(cols)]


def transposing(which):
    pairs = []
    for y, x, z, k in every():
        place = [i for i in range(4) if (OWNER[i], GROUP[i]) == (x % 2, k)][0]
        pairs.append((device(y, x, z, k), device(z - y + LIFTS[k][which], place - 2 * (x // 2), y, x // 2)))
    return pairs


def send(value, pairs):
    return lax.ppermute(value, AXES, pairs)


def split(value):
    high = value.astype(BF16)
    return high, (value - high.astype(F32)).astype(BF16)


def dot3(a, b, dims):
    (a_high, a_low), (b_high, b_low) = a, b
    mul = functools.partial(lax.dot_general, dimension_numbers=(dims, ((), ())), preferred_element_type=F32)
    return mul(a_high, b_high) + (mul(a_high, b_low) + mul(a_low, b_high))


def place_kernel(row_ref, targets_ref, own, following, sibling_own, sibling_following, inverse, pieces, both):
    row = row_ref[0]
    blocks = 3
    count = targets_ref.shape[1]
    for panel in range(2):
        for slot in range(4):
            into = slice(slot * BLOCK, (slot + 1) * BLOCK)
            hits = []
            for source in range(2 * blocks):
                index = row * blocks + source
                target = targets_ref[panel, jnp.minimum(index, count - 1)]
                hits.append(jnp.logical_and(index < count, target == row * 4 + slot))
            for core, refs in enumerate(((own, following), (sibling_own, sibling_following))):
                total = jnp.zeros((own.shape[1], BLOCK), F32)
                for source, hit in enumerate(hits):
                    at = (source % blocks) * BLOCK
                    total = jnp.where(hit, refs[source // blocks][panel, :, at : at + BLOCK], total)
                pieces[core, panel, :, into] = total
                if core == 0:
                    both[panel, :, into] = total
        both[2 + panel] = inverse[panel]


def rows_kernel(info, gathered_ref, high, low, scales, weight, scale):
    for panel in range(2):
        inverse = gathered_ref[:, 2 + panel].reshape(512, 512)
        rows = gathered_ref[:, panel].reshape(512, 512)
        factor = dot3(split(inverse), split(rows), ((0,), (0,)))
        largest = jnp.max(jnp.abs(inverse), axis=1, keepdims=True)
        weight[panel] = dot3(split(inverse / largest), split(factor), ((1,), (0,)))
        scale[panel] = jnp.broadcast_to(largest, (512, BLOCK))
    for chunk in range(3):
        for group in range(2):
            pieces = []
            for which in range(2):
                for core in (group, 1 - group):
                    start = pl.multiple_of(info[8 + chunk * 4 + group * 2 + which] * 64 + core * 32, 32)
                    for panel in range(2):
                        into = len(pieces) * 32
                        pieces.append(weight[panel, pl.ds(start, 32), :])
                        scales[chunk, group, into : into + 32, :] = scale[panel, pl.ds(start, 32), :]
            high[chunk, group], low[chunk, group] = split(jnp.concatenate(pieces).T)


def product(value, at, high, low, scale):
    scaled = value.reshape(256, 512) * jnp.concatenate([scale[at]] * 4, axis=1)
    return dot3((high[at], low[at]), split(scaled), ((1,), (0,)))


def part(info, chunk, at, value, weights):
    return product(value[...], (chunk, info[4 + at]), *weights)


def add_to(out, info, at, value):
    where = pl.multiple_of(info[at] * 512, 512)
    out[:, pl.ds(where, 512)] += value


def first_kernel(info, high, low, scale, mine, mate, next_one, above, below, out):
    out[...] = jnp.zeros(out.shape, F32)
    for chunk, at, value in ((0, 0, mine), (0, 1, mate), (0, 2, next_one), (1, 0, above), (2, 0, below)):
        add_to(out, info, at, part(info, chunk, at, value, (high, low, scale)))


def last_kernel(info, high, low, scale, across, above_mate, below_mate, begun, out):
    out[...] = begun[...]
    for chunk, at, value in ((0, 3, across), (1, 1, above_mate), (2, 1, below_mate)):
        add_to(out, info, at, part(info, chunk, at, value, (high, low, scale)))


VMEM = pl.BlockSpec(memory_space=pltpu.VMEM)
SMEM = pl.BlockSpec(memory_space=pltpu.SMEM)


def body(panel, inverse, targets):
    row, col = lax.axis_index("prow"), lax.axis_index("pcol")
    y, x, z, core = row // NX, row % NX, col // NC, col % NC

    pieces, both = pl.pallas_call(
        place_kernel,
        out_shape=(jax.ShapeDtypeStruct((2, 2, 32, 512), F32), jax.ShapeDtypeStruct((4, 32, 512), F32)),
        in_specs=[SMEM] * 2 + [VMEM] * 5,
        out_specs=(VMEM, VMEM),
        name="place",
    )(
        row.reshape(1),
        targets,
        panel,
        send(panel, to_previous_row(0)),
        send(panel, to_sibling()),
        send(panel, to_previous_row(1)),
        inverse,
    )

    gathered = lax.all_gather(both, "pcol")

    mine = jnp.stack([send(pieces, transposing(0)), send(pieces, transposing(1))])
    to_mate, to_next = swapped(lambda x: x ^ 1), swapped(lambda x: 3 - x)
    mate, next_one = send(mine, to_mate), send(mine, to_next)
    above, below = send(mine, from_y(1)), send(mine, from_y(-1))
    above_mate, below_mate = send(mate, from_y(1)), send(mate, from_y(-1))
    across = send(next_one, to_mate)

    w = (x + 2 * core) & 3
    holders = jnp.stack([w, w ^ 1, 3 - w, w ^ 2])
    sources = jnp.array([step - lift for step in (0, 1, -1) for lift in LIFTS[0] + LIFTS[1]], jnp.int32)
    info = jnp.concatenate([((holders + 1) >> 1) & 1, holders >> 1, (y + z + sources) & 7])

    def kernel(run, out_shape, operands, gflop, name, scratch=()):
        return pl.pallas_call(
            run,
            out_shape=out_shape,
            in_specs=[SMEM] + [VMEM] * len(operands),
            out_specs=(VMEM,) * len(out_shape) if isinstance(out_shape, tuple) else VMEM,
            scratch_shapes=scratch,
            compiler_params=pltpu.CompilerParams(vmem_limit_bytes=28 * MIB),
            cost_estimate=pl.CostEstimate(flops=int(gflop * 1e9), bytes_accessed=4 * MIB, transcendentals=0),
            name=name,
        )(info, *operands)

    halves = jax.ShapeDtypeStruct((3, 2, 512, 256), BF16)
    scratch = [pltpu.VMEM((2, 512, 512), F32), pltpu.VMEM((2, 512, BLOCK), F32)]
    made = (halves, halves, jax.ShapeDtypeStruct((3, 2, 256, BLOCK), F32))
    weights = kernel(rows_kernel, made, (gathered,), 3.2, "rows", scratch)
    result = jax.ShapeDtypeStruct((512, 1024), F32)
    total = kernel(first_kernel, result, weights + (mine, mate, next_one, above, below), 2.0, "first")
    return kernel(last_kernel, result, weights + (across, above_mate, below_mate, total), 1.2, "last")


def solution(mesh):
    specs = (P(None, "pcol", "prow"), P(None, "pcol", None), P())
    return jax.shard_map(body, mesh=mesh, in_specs=specs, out_specs=P("prow", "pcol"), check_vma=False)
```

```python
import functools
import jax
import jax.numpy as jnp
from jax import lax
from jax.experimental import pallas as pl
from jax.experimental.pallas import tpu as pltpu
from jax.sharding import PartitionSpec as P

BLOCK = 128
NX, NZ, NC = 4, 8, 2
AXES = ("prow", "pcol")
F32, BF16 = jnp.float32, jnp.bfloat16
MIB = 1 << 20
LIFTS = ((0, 4), (2, 6))
OWNER, GROUP = (0, 1, 1, 0), (0, 0, 1, 1)


def device(y, x, z, core):
    return ((y % 8) * NX + x % NX) * NZ * NC + z * NC + core


def every():
    for y in range(8):
        for x in range(NX):
            for z in range(NZ):
                for core in range(NC):
                    yield y, x, z, core


def swapped(x_of):
    return [(device(y, x, z, k), device(y, x_of(x), z, k)) for y, x, z, k in every()]


def from_y(distance):
    return [(device(y + distance, x, z, k), device(y, x, z, k)) for y, x, z, k in every()]


def to_sibling():
    return [(device(y, x, z, k), device(y, x, z, 1 - k)) for y, x, z, k in every()]


def to_previous_row():
    rows, cols = 8 * NX, NZ * NC
    return [(r * cols + c, (r - 1) * cols + c) for r in range(1, rows) for c in range(cols)]


def transposing(which):
    pairs = []
    for y, x, z, k in every():
        place = [i for i in range(4) if (OWNER[i], GROUP[i]) == (x % 2, k)][0]
        pairs.append((device(y, x, z, k), device(z - y + LIFTS[k][which], place - 2 * (x // 2), y, x // 2)))
    return pairs


def send(value, pairs):
    return lax.ppermute(value, AXES, pairs)


def split(value):
    high = value.astype(BF16)
    return high, (value - high.astype(F32)).astype(BF16)


def dot3(a, b, dims):
    (a_high, a_low), (b_high, b_low) = a, b
    mul = functools.partial(lax.dot_general, dimension_numbers=(dims, ((), ())), preferred_element_type=F32)
    return mul(a_high, b_high) + (mul(a_high, b_low) + mul(a_low, b_high))


def place_kernel(row_ref, targets_ref, own_ref, next_ref, inverse_ref, placed_ref, both_ref):
    row = row_ref[0]
    blocks = 3
    count = targets_ref.shape[1]
    for panel in range(2):
        for slot in range(4):
            total = jnp.zeros((own_ref.shape[1], BLOCK), F32)
            for source in range(2 * blocks):
                index = row * blocks + source
                target = targets_ref[panel, jnp.minimum(index, count - 1)]
                hit = jnp.logical_and(index < count, target == row * 4 + slot)
                ref = own_ref if source < blocks else next_ref
                at = (source % blocks) * BLOCK
                total = jnp.where(hit, ref[panel, :, at : at + BLOCK], total)
            placed_ref[panel, :, slot * BLOCK : (slot + 1) * BLOCK] = total
            both_ref[panel, :, slot * BLOCK : (slot + 1) * BLOCK] = total
        both_ref[2 + panel] = inverse_ref[panel]


def rows_kernel(info, rows_ref, inverse_ref, high, low, scales, weight, scale):
    panel = pl.program_id(0)
    inverse = inverse_ref[:, 0].reshape(512, 512)
    factor = dot3(split(inverse), split(rows_ref[:, 0].reshape(512, 512)), ((0,), (0,)))
    largest = jnp.max(jnp.abs(inverse), axis=1, keepdims=True)
    weight[panel] = dot3(split(inverse / largest), split(factor), ((1,), (0,)))
    scale[panel] = jnp.broadcast_to(largest, (512, BLOCK))

    @pl.when(panel == 1)
    def _():
        for chunk in range(3):
            for group in range(2):
                pieces = []
                for which in range(2):
                    for core in (group, 1 - group):
                        start = pl.multiple_of(info[8 + chunk * 4 + group * 2 + which] * 64 + core * 32, 32)
                        for panel in range(2):
                            into = len(pieces) * 32
                            pieces.append(weight[panel, pl.ds(start, 32), :])
                            scales[chunk, group, into : into + 32, :] = scale[panel, pl.ds(start, 32), :]
                high[chunk, group], low[chunk, group] = split(jnp.concatenate(pieces).T)


def product(info, weights, parts):
    high, low, scale = weights
    total = None
    for chunk, at, ref in parts:
        group = info[4 + at]
        value = ref[...].reshape(256, 512) * jnp.concatenate([scale[chunk, group]] * 4, axis=1)
        one = dot3((high[chunk, group], low[chunk, group]), split(value), ((1,), (0,)))
        total = one if total is None else total + one
    return total


def first_kernel(info, high, low, scale, mine, mate, next_one, above, below, out):
    weights = high, low, scale
    at, other = pl.multiple_of(info[0] * 512, 512), pl.multiple_of(info[1] * 512, 512)
    out[:, pl.ds(at, 512)] = product(info, weights, ((0, 0, mine), (0, 2, next_one), (1, 0, above), (2, 0, below)))
    out[:, pl.ds(other, 512)] = product(info, weights, ((0, 1, mate),))


def last_kernel(info, high, low, scale, across, above_mate, below_mate, begun, out):
    parts = (0, 3, across), (1, 1, above_mate), (2, 1, below_mate)
    out[...] = begun[...]
    out[:, pl.ds(pl.multiple_of(info[1] * 512, 512), 512)] += product(info, (high, low, scale), parts)


VMEM = pl.BlockSpec(memory_space=pltpu.VMEM)
SMEM = pl.BlockSpec(memory_space=pltpu.SMEM)


def body(panel, inverse, targets):
    row, col = lax.axis_index("prow"), lax.axis_index("pcol")
    y, x, z, core = row // NX, row % NX, col // NC, col % NC

    following = send(panel, to_previous_row())
    placed, both = pl.pallas_call(
        place_kernel,
        out_shape=(jax.ShapeDtypeStruct((2, 32, 512), F32), jax.ShapeDtypeStruct((4, 32, 512), F32)),
        in_specs=[SMEM, SMEM, VMEM, VMEM, VMEM],
        out_specs=(VMEM, VMEM),
        name="place",
    )(row.reshape(1), targets, panel, following, inverse)

    gathered = lax.all_gather(both, "pcol")

    pieces = jnp.stack([placed, send(placed, to_sibling())])
    mine = jnp.stack([send(pieces, transposing(0)), send(pieces, transposing(1))])
    to_mate, to_next = swapped(lambda x: x ^ 1), swapped(lambda x: 3 - x)
    mate, next_one = send(mine, to_mate), send(mine, to_next)
    above, below = send(mine, from_y(1)), send(mine, from_y(-1))
    above_mate, below_mate = send(mate, from_y(1)), send(mate, from_y(-1))
    across = send(next_one, to_mate)

    w = (x + 2 * core) & 3
    holders = jnp.stack([w, w ^ 1, 3 - w, w ^ 2])
    sources = jnp.array([step - lift for step in (0, 1, -1) for lift in LIFTS[0] + LIFTS[1]], jnp.int32)
    info = jnp.concatenate([((holders + 1) >> 1) & 1, holders >> 1, (y + z + sources) & 7])

    def kernel(run, out_shape, operands, gflop, name, **more):
        return pl.pallas_call(
            run,
            out_shape=out_shape,
            compiler_params=pltpu.CompilerParams(vmem_limit_bytes=28 * MIB),
            cost_estimate=pl.CostEstimate(flops=int(gflop * 1e9), bytes_accessed=4 * MIB, transcendentals=0),
            name=name,
            **more,
        )(info, *operands)

    halves = jax.ShapeDtypeStruct((3, 2, 512, 256), BF16)
    made = (halves, halves, jax.ShapeDtypeStruct((3, 2, 256, BLOCK), F32))
    weights = kernel(
        rows_kernel,
        made,
        (gathered, gathered),
        3.2,
        "rows",
        grid=(2,),
        in_specs=[
            SMEM,
            pl.BlockSpec((16, 1, 32, 512), lambda panel: (0, panel, 0, 0)),
            pl.BlockSpec((16, 1, 32, 512), lambda panel: (0, panel + 2, 0, 0)),
        ],
        out_specs=[pl.BlockSpec(one.shape, lambda panel, rank=len(one.shape): (0,) * rank) for one in made],
        scratch_shapes=[pltpu.VMEM((2, 512, 512), F32), pltpu.VMEM((2, 512, BLOCK), F32)],
    )
    result = jax.ShapeDtypeStruct((512, 1024), F32)
    total = kernel(
        first_kernel,
        result,
        (*weights, mine, mate, next_one, above, below),
        2.0,
        "first",
        in_specs=[SMEM] + [VMEM] * 8,
        out_specs=VMEM,
    )
    return kernel(
        last_kernel,
        result,
        (*weights, across, above_mate, below_mate, total),
        1.2,
        "last",
        in_specs=[SMEM] + [VMEM] * 7,
        out_specs=VMEM,
    )


def solution(mesh):
    specs = (P(None, "pcol", "prow"), P(None, "pcol", None), P())
    return jax.shard_map(body, mesh=mesh, in_specs=specs, out_specs=P("prow", "pcol"), check_vma=False)
```

```python
import functools
import jax
import jax.numpy as jnp
from jax import lax
from jax.experimental import pallas as pl
from jax.experimental.pallas import tpu as pltpu
from jax.sharding import PartitionSpec as P

BLOCK = 128
NX, NZ, NC = 4, 8, 2
AXES = ("prow", "pcol")
F32, BF16 = jnp.float32, jnp.bfloat16
MIB = 1 << 20
LIFTS = ((0, 4), (2, 6))
OWNER, GROUP = (0, 1, 1, 0), (0, 0, 1, 1)


def device(y, x, z, core):
    return ((y % 8) * NX + x % NX) * NZ * NC + z * NC + core


def every():
    for y in range(8):
        for x in range(NX):
            for z in range(NZ):
                for core in range(NC):
                    yield y, x, z, core


def swapped(x_of):
    return [(device(y, x, z, k), device(y, x_of(x), z, k)) for y, x, z, k in every()]


def from_y(distance):
    return [(device(y + distance, x, z, k), device(y, x, z, k)) for y, x, z, k in every()]


def to_sibling():
    return [(device(y, x, z, k), device(y, x, z, 1 - k)) for y, x, z, k in every()]


def to_previous_row():
    rows, cols = 8 * NX, NZ * NC
    return [(r * cols + c, (r - 1) * cols + c) for r in range(1, rows) for c in range(cols)]


def transposing(which):
    pairs = []
    for y, x, z, k in every():
        place = [i for i in range(4) if (OWNER[i], GROUP[i]) == (x % 2, k)][0]
        pairs.append((device(y, x, z, k), device(z - y + LIFTS[k][which], place - 2 * (x // 2), y, x // 2)))
    return pairs


def send(value, pairs):
    return lax.ppermute(value, AXES, pairs)


def split(value):
    high = value.astype(BF16)
    return high, (value - high.astype(F32)).astype(BF16)


def dot3(a, b, dims):
    (a_high, a_low), (b_high, b_low) = a, b
    mul = functools.partial(lax.dot_general, dimension_numbers=(dims, ((), ())), preferred_element_type=F32)
    return mul(a_high, b_high) + (mul(a_high, b_low) + mul(a_low, b_high))


def place_kernel(row_ref, targets_ref, own_ref, next_ref, inverse_ref, placed_ref, pair_ref, both_ref):
    row = row_ref[0]
    blocks = 3
    count = targets_ref.shape[1]
    for panel in range(2):
        for slot in range(4):
            total = jnp.zeros((own_ref.shape[1], BLOCK), F32)
            for source in range(2 * blocks):
                index = row * blocks + source
                target = targets_ref[panel, jnp.minimum(index, count - 1)]
                hit = jnp.logical_and(index < count, target == row * 4 + slot)
                ref = own_ref if source < blocks else next_ref
                at = (source % blocks) * BLOCK
                total = jnp.where(hit, ref[panel, :, at : at + BLOCK], total)
            placed_ref[panel, :, slot * BLOCK : (slot + 1) * BLOCK] = total
            both_ref[panel, :, slot * BLOCK : (slot + 1) * BLOCK] = total
            pair_ref[0, panel, :, slot * BLOCK : (slot + 1) * BLOCK] = total
        both_ref[2 + panel] = inverse_ref[panel]


def rows_kernel(info, rows_ref, inverse_ref, high, low, scales, weight, scale):
    panel = pl.program_id(0)
    inverse = inverse_ref[:, 0].reshape(512, 512)
    factor = dot3(split(inverse), split(rows_ref[:, 0].reshape(512, 512)), ((0,), (0,)))
    largest = jnp.max(jnp.abs(inverse), axis=1, keepdims=True)
    weight[panel] = dot3(split(inverse / largest), split(factor), ((1,), (0,)))
    scale[panel] = jnp.broadcast_to(largest, (512, BLOCK))

    @pl.when(panel == 1)
    def _():
        for chunk in range(3):
            for group in range(2):
                pieces = []
                for which in range(2):
                    for core in (group, 1 - group):
                        start = pl.multiple_of(info[8 + chunk * 4 + group * 2 + which] * 64 + core * 32, 32)
                        for panel in range(2):
                            into = len(pieces) * 32
                            pieces.append(weight[panel, pl.ds(start, 32), :])
                            scales[chunk, group, into : into + 32, :] = scale[panel, pl.ds(start, 32), :]
                high[chunk, group], low[chunk, group] = split(jnp.concatenate(pieces).T)


def product(info, weights, parts):
    high, low, scale = weights
    total = None
    for chunk, at, ref in parts:
        group = info[4 + at]
        value = ref[...].reshape(256, 512) * jnp.concatenate([scale[chunk, group]] * 4, axis=1)
        one = dot3((high[chunk, group], low[chunk, group]), split(value), ((1,), (0,)))
        total = one if total is None else total + one
    return total


def first_kernel(info, high, low, scale, mine, mate, next_one, above, below, out):
    weights = high, low, scale
    at, other = pl.multiple_of(info[0] * 512, 512), pl.multiple_of(info[1] * 512, 512)
    out[:, pl.ds(at, 512)] = product(info, weights, ((0, 0, mine), (0, 2, next_one), (1, 0, above), (2, 0, below)))
    out[:, pl.ds(other, 512)] = product(info, weights, ((0, 1, mate),))


def last_kernel(info, high, low, scale, across, above_mate, below_mate, begun, out):
    parts = (0, 3, across), (1, 1, above_mate), (2, 1, below_mate)
    at, other = pl.multiple_of(info[0] * 512, 512), pl.multiple_of(info[1] * 512, 512)
    out[:, pl.ds(at, 512)] = begun[:, pl.ds(at, 512)]
    out[:, pl.ds(other, 512)] = begun[:, pl.ds(other, 512)] + product(info, (high, low, scale), parts)


VMEM = pl.BlockSpec(memory_space=pltpu.VMEM)
SMEM = pl.BlockSpec(memory_space=pltpu.SMEM)


def body(panel, inverse, targets):
    row, col = lax.axis_index("prow"), lax.axis_index("pcol")
    y, x, z, core = row // NX, row % NX, col // NC, col % NC

    following = send(panel, to_previous_row())
    placed, pieces, both = pl.pallas_call(
        place_kernel,
        out_shape=tuple(jax.ShapeDtypeStruct(shape, F32) for shape in ((2, 32, 512), (2, 2, 32, 512), (4, 32, 512))),
        in_specs=[SMEM, SMEM, VMEM, VMEM, VMEM],
        out_specs=(VMEM, VMEM, VMEM),
        name="place",
    )(row.reshape(1), targets, panel, following, inverse)

    gathered = lax.all_gather(both, "pcol")

    pieces = lax.dynamic_update_slice(pieces, send(placed, to_sibling())[None], (1, 0, 0, 0))
    mine = jnp.stack([send(pieces, transposing(0)), send(pieces, transposing(1))])
    to_mate, to_next = swapped(lambda x: x ^ 1), swapped(lambda x: 3 - x)
    mate, next_one = send(mine, to_mate), send(mine, to_next)
    above, below = send(mine, from_y(1)), send(mine, from_y(-1))
    above_mate, below_mate = send(mate, from_y(1)), send(mate, from_y(-1))
    across = send(next_one, to_mate)

    w = (x + 2 * core) & 3
    holders = jnp.stack([w, w ^ 1, 3 - w, w ^ 2])
    sources = jnp.array([step - lift for step in (0, 1, -1) for lift in LIFTS[0] + LIFTS[1]], jnp.int32)
    info = jnp.concatenate([((holders + 1) >> 1) & 1, holders >> 1, (y + z + sources) & 7])

    def kernel(run, out_shape, operands, gflop, name, **more):
        return pl.pallas_call(
            run,
            out_shape=out_shape,
            compiler_params=pltpu.CompilerParams(vmem_limit_bytes=28 * MIB),
            cost_estimate=pl.CostEstimate(flops=int(gflop * 1e9), bytes_accessed=4 * MIB, transcendentals=0),
            name=name,
            **more,
        )(info, *operands)

    halves = jax.ShapeDtypeStruct((3, 2, 512, 256), BF16)
    made = (halves, halves, jax.ShapeDtypeStruct((3, 2, 256, BLOCK), F32))
    weights = kernel(
        rows_kernel,
        made,
        (gathered, gathered),
        3.2,
        "rows",
        grid=(2,),
        in_specs=[
            SMEM,
            pl.BlockSpec((16, 1, 32, 512), lambda panel: (0, panel, 0, 0)),
            pl.BlockSpec((16, 1, 32, 512), lambda panel: (0, panel + 2, 0, 0)),
        ],
        out_specs=[pl.BlockSpec(one.shape, lambda panel, rank=len(one.shape): (0,) * rank) for one in made],
        scratch_shapes=[pltpu.VMEM((2, 512, 512), F32), pltpu.VMEM((2, 512, BLOCK), F32)],
    )
    result = jax.ShapeDtypeStruct((512, 1024), F32)
    total = kernel(
        first_kernel,
        result,
        (*weights, mine, mate, next_one, above, below),
        2.0,
        "first",
        in_specs=[SMEM] + [VMEM] * 8,
        out_specs=VMEM,
    )
    return kernel(
        last_kernel,
        result,
        (*weights, across, above_mate, below_mate, total),
        1.2,
        "last",
        in_specs=[SMEM] + [VMEM] * 7,
        out_specs=VMEM,
    )


def solution(mesh):
    specs = (P(None, "pcol", "prow"), P(None, "pcol", None), P())
    return jax.shard_map(body, mesh=mesh, in_specs=specs, out_specs=P("prow", "pcol"), check_vma=False)
```

```python
import functools
import jax
import jax.numpy as jnp
from jax import lax
from jax.experimental import pallas as pl
from jax.experimental.pallas import tpu as pltpu
from jax.sharding import PartitionSpec as P

BLOCK = 128
NX, NZ, NC = 4, 8, 2
AXES = ("prow", "pcol")
F32, BF16 = jnp.float32, jnp.bfloat16
MIB = 1 << 20
LIFTS = ((0, 4), (2, 6))
OWNER, GROUP = (0, 1, 1, 0), (0, 0, 1, 1)


def device(y, x, z, core):
    return ((y % 8) * NX + x % NX) * NZ * NC + z * NC + core


def every():
    for y in range(8):
        for x in range(NX):
            for z in range(NZ):
                for core in range(NC):
                    yield y, x, z, core


def swapped(x_of):
    return [(device(y, x, z, k), device(y, x_of(x), z, k)) for y, x, z, k in every()]


def from_y(distance):
    return [(device(y + distance, x, z, k), device(y, x, z, k)) for y, x, z, k in every()]


def to_sibling():
    return [(device(y, x, z, k), device(y, x, z, 1 - k)) for y, x, z, k in every()]


def to_previous_row():
    rows, cols = 8 * NX, NZ * NC
    return [(r * cols + c, (r - 1) * cols + c) for r in range(1, rows) for c in range(cols)]


def transposing(which):
    pairs = []
    for y, x, z, k in every():
        place = [i for i in range(4) if (OWNER[i], GROUP[i]) == (x % 2, k)][0]
        pairs.append((device(y, x, z, k), device(z - y + LIFTS[k][which], place - 2 * (x // 2), y, x // 2)))
    return pairs


def send(value, pairs):
    return lax.ppermute(value, AXES, pairs)


def split(value):
    high = value.astype(BF16)
    return high, (value - high.astype(F32)).astype(BF16)


def dot3(a, b, dims):
    (a_high, a_low), (b_high, b_low) = a, b
    mul = functools.partial(lax.dot_general, dimension_numbers=(dims, ((), ())), preferred_element_type=F32)
    return mul(a_high, b_high) + (mul(a_high, b_low) + mul(a_low, b_high))


def place_kernel(row_ref, targets_ref, own_ref, next_ref, inverse_ref, placed_ref, pair_ref, both_ref):
    row = row_ref[0]
    blocks = 3
    count = targets_ref.shape[1]
    for panel in range(2):
        for slot in range(4):
            total = jnp.zeros((own_ref.shape[1], BLOCK), F32)
            for source in range(2 * blocks):
                index = row * blocks + source
                target = targets_ref[panel, jnp.minimum(index, count - 1)]
                hit = jnp.logical_and(index < count, target == row * 4 + slot)
                ref = own_ref if source < blocks else next_ref
                at = (source % blocks) * BLOCK
                total = jnp.where(hit, ref[panel, :, at : at + BLOCK], total)
            placed_ref[panel, :, slot * BLOCK : (slot + 1) * BLOCK] = total
            both_ref[panel, :, slot * BLOCK : (slot + 1) * BLOCK] = total
            pair_ref[0, panel, :, slot * BLOCK : (slot + 1) * BLOCK] = total
        both_ref[2 + panel] = inverse_ref[panel]


def rows_kernel(info, rows_ref, inverse_ref, high, low, scales, weight, scale):
    panel = pl.program_id(0)
    inverse = inverse_ref[:, 0].reshape(512, 512)
    factor = dot3(split(inverse), split(rows_ref[:, 0].reshape(512, 512)), ((0,), (0,)))
    largest = jnp.max(jnp.abs(inverse), axis=1, keepdims=True)
    weight[panel] = dot3(split(inverse / largest), split(factor), ((1,), (0,)))
    scale[panel] = jnp.broadcast_to(largest, (512, BLOCK))

    @pl.when(panel == 1)
    def _():
        for chunk in range(3):
            for group in range(2):
                pieces = []
                for which in range(2):
                    for core in (group, 1 - group):
                        start = pl.multiple_of(info[8 + chunk * 4 + group * 2 + which] * 64 + core * 32, 32)
                        for panel in range(2):
                            into = len(pieces) * 32
                            pieces.append(weight[panel, pl.ds(start, 32), :])
                            scales[chunk, group, into : into + 32, :] = scale[panel, pl.ds(start, 32), :]
                high[chunk, group], low[chunk, group] = split(jnp.concatenate(pieces).T)


def product(info, weights, parts, columns=slice(0, 512)):
    high, low, scale = weights
    total = None
    for chunk, at, ref in parts:
        group = info[4 + at]
        wide = columns.stop - columns.start
        value = ref[..., columns].reshape(256, wide) * jnp.concatenate([scale[chunk, group]] * (wide // BLOCK), axis=1)
        one = dot3((high[chunk, group], low[chunk, group]), split(value), ((1,), (0,)))
        total = one if total is None else total + one
    return total


def first_kernel(info, high, low, scale, mine, mate, next_one, above, below, out):
    weights = high, low, scale
    at, other = pl.multiple_of(info[0] * 512, 512), pl.multiple_of(info[1] * 512, 512)
    out[:, pl.ds(at, 512)] = product(info, weights, ((0, 0, mine), (0, 2, next_one), (1, 0, above), (2, 0, below)))
    out[:, pl.ds(other, 512)] = product(info, weights, ((0, 1, mate),))


def last_kernel(info, high, low, scale, across, above_mate, below_mate, begun, out, held, sems):
    parts = (0, 3, across), (1, 1, above_mate), (2, 1, below_mate)
    at, other = pl.multiple_of(info[0] * 512, 512), pl.multiple_of(info[1] * 512, 512)
    finished = pl.ds(at, 512)
    copies = [pltpu.make_async_copy(begun.at[:, finished], out.at[:, finished], sems.at[2])]
    copies[0].start()
    for piece in range(2):
        columns, into = slice(piece * 256, piece * 256 + 256), pl.ds(other + piece * 256, 256)
        held[piece] = begun[:, into] + product(info, (high, low, scale), parts, columns)
        copies.append(pltpu.make_async_copy(held.at[piece], out.at[:, into], sems.at[piece]))
        copies[-1].start()
    for copy in copies:
        copy.wait()


VMEM = pl.BlockSpec(memory_space=pltpu.VMEM)
SMEM = pl.BlockSpec(memory_space=pltpu.SMEM)


def body(panel, inverse, targets):
    row, col = lax.axis_index("prow"), lax.axis_index("pcol")
    y, x, z, core = row // NX, row % NX, col // NC, col % NC

    following = send(panel, to_previous_row())
    placed, pieces, both = pl.pallas_call(
        place_kernel,
        out_shape=tuple(jax.ShapeDtypeStruct(shape, F32) for shape in ((2, 32, 512), (2, 2, 32, 512), (4, 32, 512))),
        in_specs=[SMEM, SMEM, VMEM, VMEM, VMEM],
        out_specs=(VMEM, VMEM, VMEM),
        name="place",
    )(row.reshape(1), targets, panel, following, inverse)

    gathered = lax.all_gather(both, "pcol")

    pieces = lax.dynamic_update_slice(pieces, send(placed, to_sibling())[None], (1, 0, 0, 0))
    mine = jnp.stack([send(pieces, transposing(0)), send(pieces, transposing(1))])
    to_mate, to_next = swapped(lambda x: x ^ 1), swapped(lambda x: 3 - x)
    mate, next_one = send(mine, to_mate), send(mine, to_next)
    above, below = send(mine, from_y(1)), send(mine, from_y(-1))
    above_mate, below_mate = send(mate, from_y(1)), send(mate, from_y(-1))
    across = send(next_one, to_mate)

    w = (x + 2 * core) & 3
    holders = jnp.stack([w, w ^ 1, 3 - w, w ^ 2])
    sources = jnp.array([step - lift for step in (0, 1, -1) for lift in LIFTS[0] + LIFTS[1]], jnp.int32)
    info = jnp.concatenate([((holders + 1) >> 1) & 1, holders >> 1, (y + z + sources) & 7])

    def kernel(run, out_shape, operands, gflop, name, **more):
        return pl.pallas_call(
            run,
            out_shape=out_shape,
            compiler_params=pltpu.CompilerParams(vmem_limit_bytes=28 * MIB),
            cost_estimate=pl.CostEstimate(flops=int(gflop * 1e9), bytes_accessed=4 * MIB, transcendentals=0),
            name=name,
            **more,
        )(info, *operands)

    halves = jax.ShapeDtypeStruct((3, 2, 512, 256), BF16)
    made = (halves, halves, jax.ShapeDtypeStruct((3, 2, 256, BLOCK), F32))
    weights = kernel(
        rows_kernel,
        made,
        (gathered, gathered),
        3.2,
        "rows",
        grid=(2,),
        in_specs=[
            SMEM,
            pl.BlockSpec((16, 1, 32, 512), lambda panel: (0, panel, 0, 0)),
            pl.BlockSpec((16, 1, 32, 512), lambda panel: (0, panel + 2, 0, 0)),
        ],
        out_specs=[pl.BlockSpec(one.shape, lambda panel, rank=len(one.shape): (0,) * rank) for one in made],
        scratch_shapes=[pltpu.VMEM((2, 512, 512), F32), pltpu.VMEM((2, 512, BLOCK), F32)],
    )
    result = jax.ShapeDtypeStruct((512, 1024), F32)
    total = kernel(
        first_kernel,
        result,
        (*weights, mine, mate, next_one, above, below),
        2.0,
        "first",
        in_specs=[SMEM] + [VMEM] * 8,
        out_specs=VMEM,
    )
    return kernel(
        last_kernel,
        result,
        (*weights, across, above_mate, below_mate, total),
        1.2,
        "last",
        in_specs=[SMEM] + [VMEM] * 7,
        out_specs=pl.BlockSpec(memory_space=pl.ANY),
        scratch_shapes=[pltpu.VMEM((2, 512, 256), F32), pltpu.SemaphoreType.DMA((3,))],
    )


def solution(mesh):
    specs = (P(None, "pcol", "prow"), P(None, "pcol", None), P())
    return jax.shard_map(body, mesh=mesh, in_specs=specs, out_specs=P("prow", "pcol"), check_vma=False)
```

```python
import functools
import jax
import jax.numpy as jnp
from jax import lax
from jax.experimental import pallas as pl
from jax.experimental.pallas import tpu as pltpu
from jax.sharding import PartitionSpec as P

BLOCK = 128
NX, NZ, NC = 4, 8, 2
AXES = ("prow", "pcol")
F32, BF16 = jnp.float32, jnp.bfloat16
MIB = 1 << 20
LIFTS = ((0, 4), (6, 2))
OWNER, GROUP = (0, 1, 1, 0), (0, 0, 1, 1)


def device(y, x, z, core):
    return ((y % 8) * NX + x % NX) * NZ * NC + z * NC + core


def every():
    for y in range(8):
        for x in range(NX):
            for z in range(NZ):
                for core in range(NC):
                    yield y, x, z, core


def swapped(x_of):
    return [(device(y, x, z, k), device(y, x_of(x), z, k)) for y, x, z, k in every()]


def from_y(distance):
    return [(device(y + distance, x, z, k), device(y, x, z, k)) for y, x, z, k in every()]


def to_sibling():
    return [(device(y, x, z, k), device(y, x, z, 1 - k)) for y, x, z, k in every()]


def to_previous_row():
    rows, cols = 8 * NX, NZ * NC
    return [(r * cols + c, (r - 1) * cols + c) for r in range(1, rows) for c in range(cols)]


def transposing(which):
    pairs = []
    for y, x, z, k in every():
        place = [i for i in range(4) if (OWNER[i], GROUP[i]) == (x % 2, k)][0]
        pairs.append((device(y, x, z, k), device(z - y + LIFTS[k][which], place - 2 * (x // 2), y, x // 2)))
    return pairs


def send(value, pairs):
    return lax.ppermute(value, AXES, pairs)


def split(value):
    high = value.astype(BF16)
    return high, (value - high.astype(F32)).astype(BF16)


def dot3(a, b, dims):
    (a_high, a_low), (b_high, b_low) = a, b
    mul = functools.partial(lax.dot_general, dimension_numbers=(dims, ((), ())), preferred_element_type=F32)
    return mul(a_high, b_high) + (mul(a_high, b_low) + mul(a_low, b_high))


def place_kernel(row_ref, targets_ref, own_ref, next_ref, inverse_ref, placed_ref, both_ref):
    row = row_ref[0]
    blocks = 3
    count = targets_ref.shape[1]
    for panel in range(2):
        for slot in range(4):
            total = jnp.zeros((own_ref.shape[1], BLOCK), F32)
            for source in range(2 * blocks):
                index = row * blocks + source
                target = targets_ref[panel, jnp.minimum(index, count - 1)]
                hit = jnp.logical_and(index < count, target == row * 4 + slot)
                ref = own_ref if source < blocks else next_ref
                at = (source % blocks) * BLOCK
                total = jnp.where(hit, ref[panel, :, at : at + BLOCK], total)
            placed_ref[panel, :, slot * BLOCK : (slot + 1) * BLOCK] = total
            both_ref[panel, :, slot * BLOCK : (slot + 1) * BLOCK] = total
        both_ref[2 + panel] = inverse_ref[panel]


def rows_kernel(info, rows_ref, inverse_ref, high, low, scales, weight, scale):
    panel = pl.program_id(0)
    inverse = inverse_ref[:, 0].reshape(512, 512)
    factor = dot3(split(inverse), split(rows_ref[:, 0].reshape(512, 512)), ((0,), (0,)))
    largest = jnp.max(jnp.abs(inverse), axis=1, keepdims=True)
    weight[panel] = dot3(split(inverse / largest), split(factor), ((1,), (0,)))
    scale[panel] = jnp.broadcast_to(largest, (512, BLOCK))

    @pl.when(panel == 1)
    def _():
        for chunk in range(3):
            for group in range(2):
                pieces = []
                for which in range(2):
                    for core in (group, 1 - group):
                        start = pl.multiple_of(info[8 + chunk * 4 + group * 2 + which] * 64 + core * 32, 32)
                        for panel in range(2):
                            into = len(pieces) * 32
                            pieces.append(weight[panel, pl.ds(start, 32), :])
                            scales[chunk, group, into : into + 32, :] = scale[panel, pl.ds(start, 32), :]
                high[chunk, group], low[chunk, group] = split(jnp.concatenate(pieces).T)


def product(info, weights, parts):
    high, low, scale = weights
    total = None
    for chunk, at, ref in parts:
        group = info[4 + at]
        value = ref[...].reshape(256, 512) * jnp.concatenate([scale[chunk, group]] * 4, axis=1)
        one = dot3((high[chunk, group], low[chunk, group]), split(value), ((1,), (0,)))
        total = one if total is None else total + one
    return total


def first_kernel(info, high, low, scale, mine, mate, next_one, above, below, out):
    weights = high, low, scale
    at, other = pl.multiple_of(info[0] * 512, 512), pl.multiple_of(info[1] * 512, 512)
    out[:, pl.ds(at, 512)] = product(info, weights, ((0, 0, mine), (0, 2, next_one), (1, 0, above), (2, 0, below)))
    out[:, pl.ds(other, 512)] = product(info, weights, ((0, 1, mate),))


def last_kernel(info, high, low, scale, across, above_mate, below_mate, begun, out):
    parts = (0, 3, across), (1, 1, above_mate), (2, 1, below_mate)
    out[...] = begun[...]
    out[:, pl.ds(pl.multiple_of(info[1] * 512, 512), 512)] += product(info, (high, low, scale), parts)


VMEM = pl.BlockSpec(memory_space=pltpu.VMEM)
SMEM = pl.BlockSpec(memory_space=pltpu.SMEM)


def body(panel, inverse, targets):
    row, col = lax.axis_index("prow"), lax.axis_index("pcol")
    y, x, z, core = row // NX, row % NX, col // NC, col % NC

    following = send(panel, to_previous_row())
    placed, both = pl.pallas_call(
        place_kernel,
        out_shape=(jax.ShapeDtypeStruct((2, 32, 512), F32), jax.ShapeDtypeStruct((4, 32, 512), F32)),
        in_specs=[SMEM, SMEM, VMEM, VMEM, VMEM],
        out_specs=(VMEM, VMEM),
        name="place",
    )(row.reshape(1), targets, panel, following, inverse)

    gathered = lax.all_gather(both, "pcol")

    pieces = jnp.stack([placed, send(placed, to_sibling())])
    mine = jnp.stack([send(pieces, transposing(0)), send(pieces, transposing(1))])
    to_mate, to_next = swapped(lambda x: x ^ 1), swapped(lambda x: 3 - x)
    mate, next_one = send(mine, to_mate), send(mine, to_next)
    above, below = send(mine, from_y(1)), send(mine, from_y(-1))
    above_mate, below_mate = send(mate, from_y(1)), send(mate, from_y(-1))
    across = send(next_one, to_mate)

    w = (x + 2 * core) & 3
    holders = jnp.stack([w, w ^ 1, 3 - w, w ^ 2])
    sources = jnp.array([step - lift for step in (0, 1, -1) for lift in LIFTS[0] + LIFTS[1]], jnp.int32)
    info = jnp.concatenate([((holders + 1) >> 1) & 1, holders >> 1, (y + z + sources) & 7])

    def kernel(run, out_shape, operands, gflop, name, **more):
        return pl.pallas_call(
            run,
            out_shape=out_shape,
            compiler_params=pltpu.CompilerParams(vmem_limit_bytes=28 * MIB),
            cost_estimate=pl.CostEstimate(flops=int(gflop * 1e9), bytes_accessed=4 * MIB, transcendentals=0),
            name=name,
            **more,
        )(info, *operands)

    halves = jax.ShapeDtypeStruct((3, 2, 512, 256), BF16)
    made = (halves, halves, jax.ShapeDtypeStruct((3, 2, 256, BLOCK), F32))
    weights = kernel(
        rows_kernel,
        made,
        (gathered, gathered),
        3.2,
        "rows",
        grid=(2,),
        in_specs=[
            SMEM,
            pl.BlockSpec((16, 1, 32, 512), lambda panel: (0, panel, 0, 0)),
            pl.BlockSpec((16, 1, 32, 512), lambda panel: (0, panel + 2, 0, 0)),
        ],
        out_specs=[pl.BlockSpec(one.shape, lambda panel, rank=len(one.shape): (0,) * rank) for one in made],
        scratch_shapes=[pltpu.VMEM((2, 512, 512), F32), pltpu.VMEM((2, 512, BLOCK), F32)],
    )
    result = jax.ShapeDtypeStruct((512, 1024), F32)
    total = kernel(
        first_kernel,
        result,
        (*weights, mine, mate, next_one, above, below),
        2.0,
        "first",
        in_specs=[SMEM] + [VMEM] * 8,
        out_specs=VMEM,
    )
    return kernel(
        last_kernel,
        result,
        (*weights, across, above_mate, below_mate, total),
        1.2,
        "last",
        in_specs=[SMEM] + [VMEM] * 7,
        out_specs=VMEM,
    )


def solution(mesh):
    specs = (P(None, "pcol", "prow"), P(None, "pcol", None), P())
    return jax.shard_map(body, mesh=mesh, in_specs=specs, out_specs=P("prow", "pcol"), check_vma=False)
```
